32 devices in a mesh: dp: 4 (over y, core), head: 2 (over x), blk: 4 (over z).
Axes of the slice: x: 2, y: 2, z: 4, core: 2. Of those that a mesh axis runs over, the one named last changes fastest.
Arguments:
- queries: bfloat16 [4, 1024, 8192], P('dp', ('blk', 'head')), may hold values from -6 to 6
- keys: bfloat16 [4, 1024, 1024], P('dp', ('blk', 'head')), may hold values from -6 to 6
- values: bfloat16 [4, 1024, 1024], P('dp', ('blk', 'head')), may hold values from -6 to 6
- attention_output: bfloat16 [4, 1024, 8192], P('dp', ('blk', 'head')), may hold values from -6 to 6
- output_gradient: bfloat16 [4, 1024, 8192], P('dp', ('blk', 'head')), may hold values from -6 to 6
- saved_log_normaliser: float32 [4, 64, 1024], P('dp', 'head', 'blk')
- proj_grad: bfloat16 [4, 1024, 4096], P('dp', ('blk', 'head')), may hold values from -0.125 to 0.125
- doc_lengths: int32 [4, 8], P('dp'), may hold values from 1 to 256, as said below
Outputs:
- d_queries: bfloat16 [4, 1024, 8192], P('dp', ('blk', 'head'))
- d_keys: bfloat16 [4, 1024, 1024], P('dp', ('blk', 'head'))
- d_values: bfloat16 [4, 1024, 1024], P('dp', ('blk', 'head'))
- d_wo: bfloat16 [8192, 4096], P('head', ('dp', 'blk'))
The draws below stay inside these ranges and needn't reach their ends.
Inputs may be any that keep to these rules, and one draw needn't show every extreme that they name: `doc_lengths`: the 8 lengths of a row sum to 1024; every row holds exactly one document of 256 tokens.
All inputs are finite; a program needn't handle non-finite values.
Results may differ from the reference program's by a relative error of at most 0.014.
Values may be sent and summed in bfloat16 or wider, within the bound.
A program may use at most 192 MiB of HBM per device.

```python
import math
import jax
import jax.numpy as jnp
from jax import lax

HEAD_DIM = 128
QUERY_HEADS = 64
KEY_VALUE_HEADS = 8
DW = 4096
SEG = 256
ROW_TOKENS = 1024
PACKED_ROWS = 4
NDOC = 8
DOC_MOST = 256
N_BLK = 4


def doc_sizes(key):
    remain = ROW_TOKENS - DOC_MOST
    pieces = NDOC - 1
    spacing = remain // pieces
    jitter = spacing * 2 // 5
    inner = jnp.arange(1, pieces, dtype=jnp.int32)
    base = inner * remain // pieces
    key_cut, key_place = jax.random.split(key)
    moved = jax.random.randint(key_cut, (PACKED_ROWS, pieces - 1), -jitter, jitter + 1, dtype=jnp.int32)
    cuts = base[None, :] + moved
    first = jnp.zeros((PACKED_ROWS, 1), jnp.int32)
    final = jnp.full((PACKED_ROWS, 1), remain, jnp.int32)
    edges = jnp.concatenate([first, cuts, final], axis=1)
    parts = edges[:, 1:] - edges[:, :-1]
    longest = jax.random.randint(key_place, (PACKED_ROWS, 1), 0, NDOC, dtype=jnp.int32)
    slots = jnp.broadcast_to(jnp.arange(NDOC, dtype=jnp.int32)[None, :], (PACKED_ROWS, NDOC))
    before = jnp.take_along_axis(parts, jnp.clip(slots, 0, pieces - 1), axis=1)
    after = jnp.take_along_axis(parts, jnp.clip(slots - 1, 0, pieces - 1), axis=1)
    return jnp.where(slots < longest, before, jnp.where(slots == longest, DOC_MOST, after)).astype(jnp.int32)


def draw_doc_lengths(key, part):
    return doc_sizes(jax.random.fold_in(key, 11))


def draw_saved_log_normaliser(key, part):
    lengths = doc_sizes(jax.random.fold_in(key, 11))
    endings = jnp.cumsum(lengths, axis=1)
    positions = jnp.arange(ROW_TOKENS, dtype=jnp.int32)
    finished = positions[None, :, None] >= endings[:, None, :]
    begins = jnp.sum(jnp.where(finished, lengths[:, None, :], 0), axis=2)
    seen = (positions[None, :] - begins + 1).astype(jnp.float32)
    noise_key = jax.random.fold_in(key, 12)
    extra = jax.random.uniform(noise_key, (PACKED_ROWS, QUERY_HEADS, ROW_TOKENS), jnp.float32, 0.2, 0.8)
    return jnp.log(seen)[:, None, :] + extra


def spiked(entries, own_key, source, target, blocks, factor):
    owner, partner = [(jnp.arange(entries.shape[dim]) // (entries.shape[dim] // blocks)).reshape([-1 if axis == dim else 1 for axis in range(entries.ndim)]) for dim in (source, target)]
    chosen = jax.random.permutation(own_key, blocks)[partner]
    strong = (owner == chosen) | (owner == (partner + blocks // 2) % blocks)
    return jnp.where(strong, factor * entries, entries)


def steps_of(stream_key, shape, cuts, low, largest):
    level, own = 1.0, jax.random.fold_in(stream_key, 6)
    for dim, blocks in cuts:
        steps = jnp.exp(jax.random.uniform(jax.random.fold_in(own, dim), (blocks,), jnp.float32, low / len(cuts), largest / len(cuts)))
        level = level * jnp.repeat(steps, shape[dim] // blocks).reshape([-1 if axis == dim else 1 for axis in range(len(shape))])
    return level


def bell_draw(key, extent, deviation, reach, cuts=(), kind=jnp.bfloat16):
    result = deviation * jax.random.normal(key, extent, jnp.float32)
    if cuts:
        result = result * steps_of(key, extent, cuts, -0.22, 0.18)
    return jnp.clip(result, -reach, reach).astype(kind)


def bell_draw_with(rng, extent, deviation, reach, cuts, heavy, kind=jnp.bfloat16):
    result = deviation * jax.random.normal(rng, extent, jnp.float32)
    if cuts:
        result = result * steps_of(rng, extent, cuts, -0.22, 0.18)
    return jnp.clip(spiked(result, jax.random.fold_in(rng, 3), *heavy), -reach, reach).astype(kind)


def setup_inputs(seed: int = 0) -> dict:
    seeds = jax.random.split(jax.random.key(seed), 9)
    queries = bell_draw(seeds[0], (PACKED_ROWS, ROW_TOKENS, QUERY_HEADS * HEAD_DIM), 1.0, 6.0, ((0, 4), (1, 8)))
    keys = bell_draw(seeds[1], (PACKED_ROWS, ROW_TOKENS, KEY_VALUE_HEADS * HEAD_DIM), 1.0, 6.0, ((0, 4), (1, 8)))
    values = bell_draw(seeds[2], (PACKED_ROWS, ROW_TOKENS, KEY_VALUE_HEADS * HEAD_DIM), 1.0, 6.0, ((0, 4), (1, 8)))
    attention_output = bell_draw(seeds[3], (PACKED_ROWS, ROW_TOKENS, QUERY_HEADS * HEAD_DIM), 1.0, 6.0, ((0, 4), (1, 8)))
    output_gradient = bell_draw(seeds[4], (PACKED_ROWS, ROW_TOKENS, QUERY_HEADS * HEAD_DIM), 1.0, 6.0, ((0, 4), (1, 8)))
    saved_log_normaliser = draw_saved_log_normaliser(jax.random.fold_in(seeds[8], 71), 0)
    proj_grad = bell_draw_with(seeds[6], (PACKED_ROWS, ROW_TOKENS, DW), (PACKED_ROWS * ROW_TOKENS) ** -0.5, 0.125, ((0, 4), (1, 8)), (1, 2, 8, 2.0))
    doc_lengths = draw_doc_lengths(jax.random.fold_in(seeds[8], 71), 0)
    return {"queries": queries, "keys": keys, "values": values, "attention_output": attention_output, "output_gradient": output_gradient, "saved_log_normaliser": saved_log_normaliser, "proj_grad": proj_grad, "doc_lengths": doc_lengths}


def document_index(lengths_row, positions):
    endings = jnp.cumsum(lengths_row)
    return lax.optimization_barrier(jnp.sum((positions[:, None] >= endings[None, :]).astype(jnp.int32), axis=1))

def reference(queries, keys, values, attention_output, output_gradient, saved_log_normaliser, proj_grad, doc_lengths):
    queries_per_group = QUERY_HEADS // KEY_VALUE_HEADS
    scale = 1.0 / math.sqrt(HEAD_DIM)
    padding_extent = 2 * SEG
    starts = jnp.arange(N_BLK, dtype=jnp.int32) * SEG
    query_list = []
    key_collection = []
    value_collection = []
    for packed_row in range(PACKED_ROWS):
        query_by_head = queries[packed_row].reshape(ROW_TOKENS, KEY_VALUE_HEADS, queries_per_group, HEAD_DIM)
        output_by_head = attention_output[packed_row].reshape(ROW_TOKENS, KEY_VALUE_HEADS, queries_per_group, HEAD_DIM)
        gradient_by_head = output_gradient[packed_row].reshape(ROW_TOKENS, KEY_VALUE_HEADS, queries_per_group, HEAD_DIM)
        key_tensor_flat = keys[packed_row].reshape(ROW_TOKENS, KEY_VALUE_HEADS, HEAD_DIM)
        value_tensor_flat = values[packed_row].reshape(ROW_TOKENS, KEY_VALUE_HEADS, HEAD_DIM)
        log_normalisers = saved_log_normaliser[packed_row].reshape(KEY_VALUE_HEADS, queries_per_group, ROW_TOKENS)
        row_dots = lax.optimization_barrier(jnp.sum(gradient_by_head.astype(jnp.float32) * output_by_head.astype(jnp.float32), axis=3))
        positions = jnp.arange(ROW_TOKENS, dtype=jnp.int32)
        documents = document_index(doc_lengths[packed_row], positions)
        key_with_padding = jnp.concatenate([jnp.zeros((padding_extent, KEY_VALUE_HEADS, HEAD_DIM), keys.dtype), key_tensor_flat], axis=0)
        value_with_padding = jnp.concatenate([jnp.zeros((padding_extent, KEY_VALUE_HEADS, HEAD_DIM), values.dtype), value_tensor_flat], axis=0)
        pos_padded = jnp.arange(ROW_TOKENS + padding_extent, dtype=jnp.int32) - padding_extent
        doc_padded = jnp.concatenate([jnp.full((padding_extent,), -1, jnp.int32), documents], axis=0)

        def segment(carry, start):
            key_gradient_total, value_gradient_total = carry
            query_block = lax.dynamic_slice_in_dim(query_by_head, start, SEG, 0)
            grad_block = lax.dynamic_slice_in_dim(gradient_by_head, start, SEG, 0)
            dots_block = lax.dynamic_slice_in_dim(row_dots, start, SEG, 0)
            norms_block = lax.dynamic_slice_in_dim(log_normalisers, start, SEG, 2)
            key_window = lax.dynamic_slice_in_dim(key_with_padding, start, 3 * SEG, 0)
            value_window = lax.dynamic_slice_in_dim(value_with_padding, start, 3 * SEG, 0)
            key_pos = lax.dynamic_slice_in_dim(pos_padded, start, 3 * SEG, 0)
            key_doc = lax.dynamic_slice_in_dim(doc_padded, start, 3 * SEG, 0)
            query_pos = start + jnp.arange(SEG, dtype=jnp.int32)
            query_doc = lax.dynamic_slice_in_dim(documents, start, SEG, 0)
            visible = (query_doc[:, None] == key_doc[None, :]) & (key_pos[None, :] <= query_pos[:, None])

            def heads_per_key_value(slot):
                query_group = query_block[:, slot].astype(jnp.float32)
                grad_group = grad_block[:, slot].astype(jnp.float32)
                key_group = key_window[:, slot].astype(jnp.float32)
                value_group = value_window[:, slot].astype(jnp.float32)
                norms_group = norms_block[slot]
                dots_group = jnp.transpose(dots_block[:, slot])
                scores = jnp.einsum('tjc,uc->jtu', query_group, key_group) * scale
                probs = jnp.where(visible[None], jnp.exp(scores - norms_group[:, :, None]), jnp.float32(0.0))
                probs_low = probs.astype(jnp.bfloat16).astype(jnp.float32)
                prob_grad = jnp.einsum('tjc,uc->jtu', grad_group, value_group)
                score_grad = (probs * (prob_grad - dots_group[:, :, None]) * scale).astype(jnp.bfloat16).astype(jnp.float32)
                query_grad = jnp.einsum('jtu,uc->tjc', score_grad, key_group)
                key_grad = jnp.einsum('jtu,tjc->uc', score_grad, query_group)
                value_grad = jnp.einsum('jtu,tjc->uc', probs_low, grad_group)
                return (query_grad, key_grad, value_grad)
            query_gradient_rows, key_gradient_rows, value_gradient_rows = lax.map(heads_per_key_value, jnp.arange(KEY_VALUE_HEADS, dtype=jnp.int32))
            query_out = jnp.transpose(query_gradient_rows, (1, 0, 2, 3)).reshape(SEG, QUERY_HEADS * HEAD_DIM)
            key_now = lax.dynamic_slice_in_dim(key_gradient_total, start, 3 * SEG, 0) + jnp.transpose(key_gradient_rows, (1, 0, 2))
            value_now = lax.dynamic_slice_in_dim(value_gradient_total, start, 3 * SEG, 0) + jnp.transpose(value_gradient_rows, (1, 0, 2))
            key_gradient_total = lax.dynamic_update_slice_in_dim(key_gradient_total, key_now, start, 0)
            value_gradient_total = lax.dynamic_update_slice_in_dim(value_gradient_total, value_now, start, 0)
            return ((key_gradient_total, value_gradient_total), query_out)
        empty_slots = jnp.zeros((ROW_TOKENS + padding_extent, KEY_VALUE_HEADS, HEAD_DIM), jnp.float32)
        (key_gradient_total, value_gradient_total), query_blocks = lax.scan(segment, (empty_slots, empty_slots), starts)
        query_list.append(query_blocks.reshape(ROW_TOKENS, QUERY_HEADS * HEAD_DIM).astype(jnp.bfloat16))
        key_collection.append(key_gradient_total[padding_extent:].reshape(ROW_TOKENS, KEY_VALUE_HEADS * HEAD_DIM).astype(jnp.bfloat16))
        value_collection.append(value_gradient_total[padding_extent:].reshape(ROW_TOKENS, KEY_VALUE_HEADS * HEAD_DIM).astype(jnp.bfloat16))

    def wo_part(total, index):
        packed_row = index // N_BLK
        start = index % N_BLK * SEG
        out_rows = lax.dynamic_slice(attention_output, (packed_row, start, jnp.int32(0)), (1, SEG, QUERY_HEADS * HEAD_DIM))[0]
        grad_rows = lax.dynamic_slice(proj_grad, (packed_row, start, jnp.int32(0)), (1, SEG, DW))[0]
        part = jnp.dot(jnp.transpose(out_rows), grad_rows, preferred_element_type=jnp.float32)
        part = lax.optimization_barrier(part.astype(jnp.bfloat16)).astype(jnp.float32)
        return (total + part, None)
    wo_total, unused = lax.scan(wo_part, jnp.zeros((QUERY_HEADS * HEAD_DIM, DW), jnp.float32), jnp.arange(PACKED_ROWS * N_BLK, dtype=jnp.int32))
    return (jnp.stack(query_list), jnp.stack(key_collection), jnp.stack(value_collection), wo_total.astype(jnp.bfloat16))
```

```python
import functools
import math

import jax
import jax.numpy as jnp
from jax import lax
from jax.experimental import pallas as pl
from jax.experimental.pallas import tpu as pltpu
from jax.sharding import PartitionSpec as P

HEAD_DIM = 128
CHUNKS = 4


def nt(left, right):
    return lax.dot_general(left, right, (((1,), (1,)), ((), ())), preferred_element_type=jnp.float32)


def tn(left, right):
    return lax.dot_general(left, right, (((0,), (0,)), ((), ())), preferred_element_type=jnp.float32)


def attention_kernel(
    halos, per_group, docs, lengths, base_ref, q_ref, g_ref, k_ref, v_ref, norm_ref, dots_ref,
    dq_ref, dk_ref, dv_ref, dk_far_ref, dv_far_ref, q_stack, g_stack, dq_acc
):
    tokens = q_ref.shape[0]
    base = base_ref[0]
    scale = 1.0 / math.sqrt(HEAD_DIM)
    for j in range(per_group):
        rows = slice(j * tokens, (j + 1) * tokens)
        cols = slice(j * HEAD_DIM, (j + 1) * HEAD_DIM)
        q_stack[rows, :] = q_ref[:, cols]
        g_stack[rows, :] = g_ref[:, cols]
    query_pos = base + lax.broadcasted_iota(jnp.int32, (tokens, tokens), 1)
    key_offset = lax.broadcasted_iota(jnp.int32, (tokens, tokens), 0)
    start = jnp.zeros((tokens, tokens), jnp.int32)
    first_start = jnp.int32(0)
    end = jnp.int32(0)
    for n in range(docs):
        end = end + lengths[n]
        start = jnp.where(query_pos >= end, end, start)
        first_start = jnp.where(base >= end, end, first_start)

    def block(back):
        rows = slice((halos - back) * tokens, (halos - back + 1) * tokens)
        key_pos = base - back * tokens + key_offset
        visible = (key_pos >= start) & (key_pos <= query_pos)
        visible = jnp.concatenate([visible.astype(jnp.float32)] * per_group, axis=1)
        keys = k_ref[rows, :]
        queries = q_stack[...]
        grads = g_stack[...]
        scores = nt(keys, queries) * scale
        probs = jnp.where(visible > 0.0, jnp.exp(scores - norm_ref[0]), 0.0)
        prob_grad = nt(v_ref[rows, :], grads)
        score_grad = (probs * (prob_grad - dots_ref[0]) * scale).astype(jnp.bfloat16)
        value_part = jnp.dot(probs.astype(jnp.bfloat16), grads, preferred_element_type=jnp.float32)
        key_part = jnp.dot(score_grad, queries, preferred_element_type=jnp.float32)
        return tn(score_grad, keys), key_part, value_part

    query_part, key_part, value_part = block(0)
    dq_acc[...] = query_part
    dk_ref[...] = key_part
    dv_ref[...] = value_part
    for back in range(1, halos + 1):
        rows = slice((halos - back) * tokens, (halos - back + 1) * tokens)
        near = base - back * tokens + tokens - 1 >= first_start

        @pl.when(near)
        def _(back=back, rows=rows):
            query_part, key_part, value_part = block(back)
            dq_acc[...] += query_part
            dk_far_ref[rows, :] = key_part.astype(dk_far_ref.dtype)
            dv_far_ref[rows, :] = value_part.astype(dv_far_ref.dtype)

        @pl.when(jnp.logical_not(near))
        def _(rows=rows):
            dk_far_ref[rows, :] = jnp.zeros((tokens, HEAD_DIM), dk_far_ref.dtype)
            dv_far_ref[rows, :] = jnp.zeros((tokens, HEAD_DIM), dv_far_ref.dtype)

    for j in range(per_group):
        rows = slice(j * tokens, (j + 1) * tokens)
        dq_ref[:, j * HEAD_DIM : (j + 1) * HEAD_DIM] = dq_acc[rows, :].astype(dq_ref.dtype)


def attention(lengths, base, queries, grads, keys, values, norms, dots, halos):
    tokens = queries.shape[0]
    groups = keys.shape[1] // HEAD_DIM
    per_group = queries.shape[1] // keys.shape[1]
    wide = per_group * HEAD_DIM
    body = functools.partial(attention_kernel, halos, per_group, lengths.shape[0])
    by_group = lambda g, *_: (0, g)
    stat = pl.BlockSpec((1, 1, per_group * tokens), lambda g, *_: (g, 0, 0))
    one = jax.ShapeDtypeStruct((tokens, groups * HEAD_DIM), jnp.float32)
    far = jax.ShapeDtypeStruct((halos * tokens, groups * HEAD_DIM), jnp.bfloat16)
    return pl.pallas_call(
        body,
        grid_spec=pltpu.PrefetchScalarGridSpec(
            num_scalar_prefetch=2,
            grid=(groups,),
            in_specs=[
                pl.BlockSpec((tokens, wide), by_group),
                pl.BlockSpec((tokens, wide), by_group),
                pl.BlockSpec((keys.shape[0], HEAD_DIM), by_group),
                pl.BlockSpec((keys.shape[0], HEAD_DIM), by_group),
                stat,
                stat,
            ],
            out_specs=[
                pl.BlockSpec((tokens, wide), by_group),
                pl.BlockSpec((tokens, HEAD_DIM), by_group),
                pl.BlockSpec((tokens, HEAD_DIM), by_group),
                pl.BlockSpec((halos * tokens, HEAD_DIM), by_group),
                pl.BlockSpec((halos * tokens, HEAD_DIM), by_group),
            ],
            scratch_shapes=[
                pltpu.VMEM((per_group * tokens, HEAD_DIM), jnp.bfloat16),
                pltpu.VMEM((per_group * tokens, HEAD_DIM), jnp.bfloat16),
                pltpu.VMEM((per_group * tokens, HEAD_DIM), jnp.float32),
            ],
        ),
        out_shape=[jax.ShapeDtypeStruct(queries.shape, jnp.bfloat16), one, one, far, far],
        compiler_params=pltpu.CompilerParams(vmem_limit_bytes=40 * 1024 * 1024),
        cost_estimate=pl.CostEstimate(
            flops=30_000_000_000, bytes_accessed=10_000_000, transcendentals=3_000_000
        ),
    )(lengths, base, queries, grads, keys, values, norms, dots)


def shifted(x, by):
    blocks, halves = lax.axis_size("blk"), lax.axis_size("head")
    place = lambda i: i % halves * blocks + i // halves
    count = blocks * halves
    pairs = [(place(i), place(i + by)) for i in range(count) if 0 <= i + by < count]
    return lax.ppermute(x, ("head", "blk"), pairs)


def shards(
    queries, keys, values, attention_output, output_gradient, saved_log_normaliser, proj_grad, doc_lengths
):
    halos = lax.axis_size("head")
    queries, keys, values = queries[0], keys[0], values[0]
    outputs, grads, cols = attention_output[0], output_gradient[0], proj_grad[0]
    tokens = queries.shape[0]
    groups = keys.shape[1] // HEAD_DIM
    heads = queries.shape[1] // HEAD_DIM

    cols = lax.all_gather(cols, "head", axis=0, tiled=True)
    cols = lax.all_to_all(cols, "dp", split_axis=1, concat_axis=0, tiled=True)
    features = outputs.shape[1] // halos
    piece = features // CHUNKS
    by_half = outputs.reshape(tokens, halos, features)

    def weight(index):
        part = by_half[:, :, index * piece : (index + 1) * piece].reshape(tokens, halos * piece)
        part = lax.all_to_all(part, "head", split_axis=1, concat_axis=0, tiled=True)
        part = lax.all_gather(part, "dp", axis=0, tiled=True)
        part = tn(part, cols).astype(jnp.bfloat16)
        return lax.psum_scatter(part, "blk", scatter_dimension=1, tiled=True)

    both = jnp.concatenate([keys, values], axis=1)
    window = [shifted(both, back) for back in range(halos, 0, -1)] + [both]
    window = jnp.concatenate(window, axis=0)
    width = keys.shape[1]
    norms = lax.all_to_all(saved_log_normaliser[0], "head", split_axis=1, concat_axis=0, tiled=True)
    dots = jnp.sum(
        (grads.astype(jnp.float32) * outputs.astype(jnp.float32)).reshape(tokens, heads, HEAD_DIM), axis=2
    )
    base = (lax.axis_index("blk") * halos + lax.axis_index("head")) * tokens
    d_queries, d_keys, d_values, far_keys, far_values = attention(
        doc_lengths[0],
        base.astype(jnp.int32)[None],
        queries,
        grads,
        window[:, :width],
        window[:, width:],
        norms.reshape(groups, 1, -1),
        dots.T.reshape(groups, 1, -1),
        halos,
    )
    for back in range(1, halos + 1):
        rows = slice((halos - back) * tokens, (halos - back + 1) * tokens)
        far = shifted(jnp.concatenate([far_keys[rows], far_values[rows]], axis=1), -back)
        d_keys = d_keys + far[:, :width].astype(jnp.float32)
        d_values = d_values + far[:, width:].astype(jnp.float32)
    d_weight = jnp.concatenate([weight(index) for index in range(CHUNKS)], axis=0)
    return (
        d_queries[None],
        d_keys.astype(jnp.bfloat16)[None],
        d_values.astype(jnp.bfloat16)[None],
        d_weight,
    )


def solution(mesh):
    tokens = P("dp", ("blk", "head"), None)
    in_specs = (tokens, tokens, tokens, tokens, tokens, P("dp", "head", "blk"), tokens, P("dp", None))
    out_specs = (tokens, tokens, tokens, P("head", ("dp", "blk")))
    return jax.shard_map(shards, mesh=mesh, in_specs=in_specs, out_specs=out_specs, check_vma=False)
```

```python
import functools
import math

import jax
import jax.numpy as jnp
from jax import lax
from jax.experimental import pallas as pl
from jax.experimental.pallas import tpu as pltpu
from jax.sharding import PartitionSpec as P

HEAD_DIM = 128
CHUNKS = 4


def nt(left, right):
    return lax.dot_general(left, right, (((1,), (1,)), ((), ())), preferred_element_type=jnp.float32)


def tn(left, right):
    return lax.dot_general(left, right, (((0,), (0,)), ((), ())), preferred_element_type=jnp.float32)


def attention_kernel(
    halos, per_group, docs, lengths, base_ref, q_ref, g_ref, k_ref, v_ref, norm_ref, dots_ref,
    dq_ref, dk_ref, dv_ref, dk_far_ref, dv_far_ref, q_stack, g_stack, dq_acc
):
    tokens = q_ref.shape[0]
    base = base_ref[0]
    scale = 1.0 / math.sqrt(HEAD_DIM)
    for j in range(per_group):
        rows = slice(j * tokens, (j + 1) * tokens)
        cols = slice(j * HEAD_DIM, (j + 1) * HEAD_DIM)
        q_stack[rows, :] = q_ref[:, cols]
        g_stack[rows, :] = g_ref[:, cols]
    query_pos = base + lax.broadcasted_iota(jnp.int32, (tokens, tokens), 1)
    key_offset = lax.broadcasted_iota(jnp.int32, (tokens, tokens), 0)
    start = jnp.zeros((tokens, tokens), jnp.int32)
    first_start = jnp.int32(0)
    end = jnp.int32(0)
    for n in range(docs):
        end = end + lengths[n]
        start = jnp.where(query_pos >= end, end, start)
        first_start = jnp.where(base >= end, end, first_start)

    def block(back):
        rows = slice((halos - back) * tokens, (halos - back + 1) * tokens)
        key_pos = base - back * tokens + key_offset
        visible = (key_pos >= start) & (key_pos <= query_pos)
        visible = jnp.concatenate([visible.astype(jnp.float32)] * per_group, axis=1)
        keys = k_ref[rows, :]
        queries = q_stack[...]
        grads = g_stack[...]
        scores = nt(keys, queries) * scale
        probs = jnp.where(visible > 0.0, jnp.exp(scores - norm_ref[0]), 0.0)
        prob_grad = nt(v_ref[rows, :], grads)
        score_grad = (probs * (prob_grad - dots_ref[0]) * scale).astype(jnp.bfloat16)
        value_part = jnp.dot(probs.astype(jnp.bfloat16), grads, preferred_element_type=jnp.float32)
        key_part = jnp.dot(score_grad, queries, preferred_element_type=jnp.float32)
        return tn(score_grad, keys), key_part, value_part

    query_part, key_part, value_part = block(0)
    dq_acc[...] = query_part
    dk_ref[...] = key_part
    dv_ref[...] = value_part
    for back in range(1, halos + 1):
        rows = slice((halos - back) * tokens, (halos - back + 1) * tokens)
        near = base - back * tokens + tokens - 1 >= first_start

        @pl.when(near)
        def _(back=back, rows=rows):
            query_part, key_part, value_part = block(back)
            dq_acc[...] += query_part
            dk_far_ref[rows, :] = key_part.astype(dk_far_ref.dtype)
            dv_far_ref[rows, :] = value_part.astype(dv_far_ref.dtype)

        @pl.when(jnp.logical_not(near))
        def _(rows=rows):
            dk_far_ref[rows, :] = jnp.zeros((tokens, HEAD_DIM), dk_far_ref.dtype)
            dv_far_ref[rows, :] = jnp.zeros((tokens, HEAD_DIM), dv_far_ref.dtype)

    for j in range(per_group):
        rows = slice(j * tokens, (j + 1) * tokens)
        dq_ref[:, j * HEAD_DIM : (j + 1) * HEAD_DIM] = dq_acc[rows, :].astype(dq_ref.dtype)


def attention(lengths, base, queries, grads, keys, values, norms, dots, halos):
    tokens = queries.shape[0]
    groups = keys.shape[1] // HEAD_DIM
    per_group = queries.shape[1] // keys.shape[1]
    wide = per_group * HEAD_DIM
    body = functools.partial(attention_kernel, halos, per_group, lengths.shape[0])
    by_group = lambda g, *_: (0, g)
    stat = pl.BlockSpec((1, 1, per_group * tokens), lambda g, *_: (g, 0, 0))
    one = jax.ShapeDtypeStruct((tokens, groups * HEAD_DIM), jnp.float32)
    far = jax.ShapeDtypeStruct((halos * tokens, groups * HEAD_DIM), jnp.bfloat16)
    return pl.pallas_call(
        body,
        grid_spec=pltpu.PrefetchScalarGridSpec(
            num_scalar_prefetch=2,
            grid=(groups,),
            in_specs=[
                pl.BlockSpec((tokens, wide), by_group),
                pl.BlockSpec((tokens, wide), by_group),
                pl.BlockSpec((keys.shape[0], HEAD_DIM), by_group),
                pl.BlockSpec((keys.shape[0], HEAD_DIM), by_group),
                stat,
                stat,
            ],
            out_specs=[
                pl.BlockSpec((tokens, wide), by_group),
                pl.BlockSpec((tokens, HEAD_DIM), by_group),
                pl.BlockSpec((tokens, HEAD_DIM), by_group),
                pl.BlockSpec((halos * tokens, HEAD_DIM), by_group),
                pl.BlockSpec((halos * tokens, HEAD_DIM), by_group),
            ],
            scratch_shapes=[
                pltpu.VMEM((per_group * tokens, HEAD_DIM), jnp.bfloat16),
                pltpu.VMEM((per_group * tokens, HEAD_DIM), jnp.bfloat16),
                pltpu.VMEM((per_group * tokens, HEAD_DIM), jnp.float32),
            ],
        ),
        out_shape=[jax.ShapeDtypeStruct(queries.shape, jnp.bfloat16), one, one, far, far],
        compiler_params=pltpu.CompilerParams(vmem_limit_bytes=40 * 1024 * 1024),
        cost_estimate=pl.CostEstimate(
            flops=30_000_000_000, bytes_accessed=10_000_000, transcendentals=3_000_000
        ),
    )(lengths, base, queries, grads, keys, values, norms, dots)


def shifted(x, by):
    blocks, halves = lax.axis_size("blk"), lax.axis_size("head")
    place = lambda i: i % halves * blocks + i // halves
    count = blocks * halves
    pairs = [(place(i), place(i + by)) for i in range(count) if 0 <= i + by < count]
    return lax.ppermute(x, ("head", "blk"), pairs)


def shards(
    queries, keys, values, attention_output, output_gradient, saved_log_normaliser, proj_grad, doc_lengths
):
    halos = lax.axis_size("head")
    queries, keys, values = queries[0], keys[0], values[0]
    outputs, grads, cols_own = attention_output[0], output_gradient[0], proj_grad[0]
    tokens = queries.shape[0]
    groups = keys.shape[1] // HEAD_DIM
    heads = queries.shape[1] // HEAD_DIM

    rows_dp = lax.axis_size("dp")
    dp_order = [0]
    bits = [rows_dp >> n for n in range(1, rows_dp.bit_length())]
    for bit in bits:
        dp_order = dp_order + [other ^ bit for other in dp_order]
    dp_index, head_index = lax.axis_index("dp"), lax.axis_index("head")
    quarter = cols_own.shape[1] // rows_dp
    features = outputs.shape[1] // halos
    piece = features // CHUNKS

    def from_head(pick):
        return jnp.concatenate(
            [pick(head_index)]
            + [
                lax.ppermute(
                    pick((head_index + k) % halos), "head", [(i, (i + k) % halos) for i in range(halos)]
                )
                for k in range(1, halos)
            ],
            axis=0,
        )

    def flipped(x, bit):
        return lax.ppermute(x, "dp", [(i, i ^ bit) for i in range(rows_dp)])

    cols = from_head(lambda h: cols_own)
    cols = jnp.concatenate(
        [
            lax.dynamic_slice_in_dim(cols, (dp_index ^ other) * quarter, quarter, 1)
            if other == 0
            else flipped(lax.dynamic_slice_in_dim(cols, (dp_index ^ other) * quarter, quarter, 1), other)
            for other in dp_order
        ],
        axis=0,
    )

    def weight(index):
        part = from_head(
            lambda h: lax.dynamic_slice_in_dim(outputs, h * features + index * piece, piece, 1)
        )
        for bit in bits:
            part = jnp.concatenate([part, flipped(part, bit)], axis=0)
        part = tn(part, cols).astype(jnp.bfloat16)
        return lax.psum_scatter(part, "blk", scatter_dimension=1, tiled=True)

    both = jnp.concatenate([keys, values], axis=1)
    window = [shifted(both, back) for back in range(halos, 0, -1)] + [both]
    window = jnp.concatenate(window, axis=0)
    width = keys.shape[1]
    norms = lax.all_to_all(saved_log_normaliser[0], "head", split_axis=1, concat_axis=0, tiled=True)
    dots = jnp.sum(
        (grads.astype(jnp.float32) * outputs.astype(jnp.float32)).reshape(tokens, heads, HEAD_DIM), axis=2
    )
    base = (lax.axis_index("blk") * halos + lax.axis_index("head")) * tokens
    d_queries, d_keys, d_values, far_keys, far_values = attention(
        doc_lengths[0],
        base.astype(jnp.int32)[None],
        queries,
        grads,
        window[:, :width],
        window[:, width:],
        norms.reshape(groups, 1, -1),
        dots.T.reshape(groups, 1, -1),
        halos,
    )
    for back in range(1, halos + 1):
        rows = slice((halos - back) * tokens, (halos - back + 1) * tokens)
        far = shifted(jnp.concatenate([far_keys[rows], far_values[rows]], axis=1), -back)
        d_keys = d_keys + far[:, :width].astype(jnp.float32)
        d_values = d_values + far[:, width:].astype(jnp.float32)
    d_weight = jnp.concatenate([weight(index) for index in range(CHUNKS)], axis=0)
    return (
        d_queries[None],
        d_keys.astype(jnp.bfloat16)[None],
        d_values.astype(jnp.bfloat16)[None],
        d_weight,
    )


def solution(mesh):
    tokens = P("dp", ("blk", "head"), None)
    in_specs = (tokens, tokens, tokens, tokens, tokens, P("dp", "head", "blk"), tokens, P("dp", None))
    out_specs = (tokens, tokens, tokens, P("head", ("dp", "blk")))
    return jax.shard_map(shards, mesh=mesh, in_specs=in_specs, out_specs=out_specs, check_vma=False)
```

```python
import functools
import math

import jax
import jax.numpy as jnp
from jax import lax
from jax.experimental import pallas as pl
from jax.experimental.pallas import tpu as pltpu
from jax.sharding import PartitionSpec as P

HEAD_DIM = 128
CHUNKS = 4


def nt(left, right):
    return lax.dot_general(left, right, (((1,), (1,)), ((), ())), preferred_element_type=jnp.float32)


def tn(left, right):
    return lax.dot_general(left, right, (((0,), (0,)), ((), ())), preferred_element_type=jnp.float32)


def attention_kernel(
    halos, per_group, docs, lengths, base_ref, q_ref, g_ref, k_ref, v_ref, norm_ref, dots_ref,
    dq_ref, dk_ref, dv_ref, dk_far_ref, dv_far_ref, q_stack, g_stack, dq_acc
):
    tokens = q_ref.shape[0]
    base = base_ref[0]
    scale = 1.0 / math.sqrt(HEAD_DIM)
    for j in range(per_group):
        rows = slice(j * tokens, (j + 1) * tokens)
        cols = slice(j * HEAD_DIM, (j + 1) * HEAD_DIM)
        q_stack[rows, :] = q_ref[:, cols]
        g_stack[rows, :] = g_ref[:, cols]
    query_pos = base + lax.broadcasted_iota(jnp.int32, (tokens, tokens), 1)
    key_offset = lax.broadcasted_iota(jnp.int32, (tokens, tokens), 0)
    start = jnp.zeros((tokens, tokens), jnp.int32)
    first_start = jnp.int32(0)
    end = jnp.int32(0)
    for n in range(docs):
        end = end + lengths[n]
        start = jnp.where(query_pos >= end, end, start)
        first_start = jnp.where(base >= end, end, first_start)

    def block(back):
        rows = slice((halos - back) * tokens, (halos - back + 1) * tokens)
        key_pos = base - back * tokens + key_offset
        visible = (key_pos >= start) & (key_pos <= query_pos)
        visible = jnp.concatenate([visible.astype(jnp.float32)] * per_group, axis=1)
        keys = k_ref[rows, :]
        queries = q_stack[...]
        grads = g_stack[...]
        scores = nt(keys, queries) * scale
        probs = jnp.where(visible > 0.0, jnp.exp(scores - norm_ref[0]), 0.0)
        prob_grad = nt(v_ref[rows, :], grads)
        score_grad = (probs * (prob_grad - dots_ref[0]) * scale).astype(jnp.bfloat16)
        value_part = jnp.dot(probs.astype(jnp.bfloat16), grads, preferred_element_type=jnp.float32)
        key_part = jnp.dot(score_grad, queries, preferred_element_type=jnp.float32)
        return tn(score_grad, keys), key_part, value_part

    query_part, key_part, value_part = block(0)
    dq_acc[...] = query_part
    dk_ref[...] = key_part
    dv_ref[...] = value_part
    for back in range(1, halos + 1):
        rows = slice((halos - back) * tokens, (halos - back + 1) * tokens)
        near = base - back * tokens + tokens - 1 >= first_start

        @pl.when(near)
        def _(back=back, rows=rows):
            query_part, key_part, value_part = block(back)
            dq_acc[...] += query_part
            dk_far_ref[rows, :] = key_part.astype(dk_far_ref.dtype)
            dv_far_ref[rows, :] = value_part.astype(dv_far_ref.dtype)

        @pl.when(jnp.logical_not(near))
        def _(rows=rows):
            dk_far_ref[rows, :] = jnp.zeros((tokens, HEAD_DIM), dk_far_ref.dtype)
            dv_far_ref[rows, :] = jnp.zeros((tokens, HEAD_DIM), dv_far_ref.dtype)

    for j in range(per_group):
        rows = slice(j * tokens, (j + 1) * tokens)
        dq_ref[:, j * HEAD_DIM : (j + 1) * HEAD_DIM] = dq_acc[rows, :].astype(dq_ref.dtype)


def attention(lengths, base, queries, grads, keys, values, norms, dots, halos):
    tokens = queries.shape[0]
    groups = keys.shape[1] // HEAD_DIM
    per_group = queries.shape[1] // keys.shape[1]
    wide = per_group * HEAD_DIM
    body = functools.partial(attention_kernel, halos, per_group, lengths.shape[0])
    by_group = lambda g, *_: (0, g)
    stat = pl.BlockSpec((1, 1, per_group * tokens), lambda g, *_: (g, 0, 0))
    one = jax.ShapeDtypeStruct((tokens, groups * HEAD_DIM), jnp.float32)
    far = jax.ShapeDtypeStruct((halos * tokens, groups * HEAD_DIM), jnp.bfloat16)
    return pl.pallas_call(
        body,
        grid_spec=pltpu.PrefetchScalarGridSpec(
            num_scalar_prefetch=2,
            grid=(groups,),
            in_specs=[
                pl.BlockSpec((tokens, wide), by_group),
                pl.BlockSpec((tokens, wide), by_group),
                pl.BlockSpec((keys.shape[0], HEAD_DIM), by_group),
                pl.BlockSpec((keys.shape[0], HEAD_DIM), by_group),
                stat,
                stat,
            ],
            out_specs=[
                pl.BlockSpec((tokens, wide), by_group),
                pl.BlockSpec((tokens, HEAD_DIM), by_group),
                pl.BlockSpec((tokens, HEAD_DIM), by_group),
                pl.BlockSpec((halos * tokens, HEAD_DIM), by_group),
                pl.BlockSpec((halos * tokens, HEAD_DIM), by_group),
            ],
            scratch_shapes=[
                pltpu.VMEM((per_group * tokens, HEAD_DIM), jnp.bfloat16),
                pltpu.VMEM((per_group * tokens, HEAD_DIM), jnp.bfloat16),
                pltpu.VMEM((per_group * tokens, HEAD_DIM), jnp.float32),
            ],
        ),
        out_shape=[jax.ShapeDtypeStruct(queries.shape, jnp.bfloat16), one, one, far, far],
        compiler_params=pltpu.CompilerParams(vmem_limit_bytes=40 * 1024 * 1024),
        cost_estimate=pl.CostEstimate(
            flops=30_000_000_000, bytes_accessed=10_000_000, transcendentals=3_000_000
        ),
    )(lengths, base, queries, grads, keys, values, norms, dots)


def shifted(x, by):
    blocks, halves = lax.axis_size("blk"), lax.axis_size("head")
    place = lambda i: i % halves * blocks + i // halves
    count = blocks * halves
    pairs = [(place(i), place(i + by)) for i in range(count) if 0 <= i + by < count]
    return lax.ppermute(x, ("head", "blk"), pairs)


def shards(
    queries, keys, values, attention_output, output_gradient, saved_log_normaliser, proj_grad, doc_lengths
):
    halos = lax.axis_size("head")
    queries, keys, values = queries[0], keys[0], values[0]
    outputs, grads, cols_own = attention_output[0], output_gradient[0], proj_grad[0]
    tokens = queries.shape[0]
    groups = keys.shape[1] // HEAD_DIM
    heads = queries.shape[1] // HEAD_DIM

    rows_dp = lax.axis_size("dp")
    dp_order = [0]
    bits = [rows_dp >> n for n in range(1, rows_dp.bit_length())]
    for bit in bits:
        dp_order = dp_order + [other ^ bit for other in dp_order]
    dp_index, head_index = lax.axis_index("dp"), lax.axis_index("head")
    quarter = cols_own.shape[1] // rows_dp
    features = outputs.shape[1] // halos
    piece = features // CHUNKS

    def from_head(pick):
        return jnp.concatenate(
            [pick(head_index)]
            + [
                lax.ppermute(
                    pick((head_index + k) % halos), "head", [(i, (i + k) % halos) for i in range(halos)]
                )
                for k in range(1, halos)
            ],
            axis=0,
        )

    def flipped(x, bit):
        return lax.ppermute(x, "dp", [(i, i ^ bit) for i in range(rows_dp)])

    cols = from_head(lambda h: cols_own)
    cols = jnp.concatenate(
        [
            lax.dynamic_slice_in_dim(cols, (dp_index ^ other) * quarter, quarter, 1)
            if other == 0
            else flipped(lax.dynamic_slice_in_dim(cols, (dp_index ^ other) * quarter, quarter, 1), other)
            for other in dp_order
        ],
        axis=0,
    )

    mine = from_head(lambda h: lax.dynamic_slice_in_dim(outputs, h * features, features, 1))
    blocks, block_index = lax.axis_size("blk"), lax.axis_index("blk")
    share = quarter // blocks

    def weight(index):
        part = mine[:, index * piece : (index + 1) * piece]
        for bit in bits:
            part = jnp.concatenate([part, flipped(part, bit)], axis=0)
        part = tn(part, cols).astype(jnp.bfloat16)
        if index % 2 == 0:
            return lax.psum_scatter(part, "blk", scatter_dimension=1, tiled=True)
        pick = lambda b: lax.dynamic_slice_in_dim(part, b * share, share, 1)
        total = pick(block_index).astype(jnp.float32)
        for k in range(1, blocks):
            pairs = [(i, (i + k) % blocks) for i in range(blocks)]
            total += lax.ppermute(pick((block_index + k) % blocks), "blk", pairs).astype(jnp.float32)
        return total.astype(jnp.bfloat16)

    both = jnp.concatenate([keys, values], axis=1)
    window = [shifted(both, back) for back in range(halos, 0, -1)] + [both]
    window = jnp.concatenate(window, axis=0)
    width = keys.shape[1]
    norms = lax.all_to_all(saved_log_normaliser[0], "head", split_axis=1, concat_axis=0, tiled=True)
    dots = jnp.sum(
        (grads.astype(jnp.float32) * outputs.astype(jnp.float32)).reshape(tokens, heads, HEAD_DIM), axis=2
    )
    base = (lax.axis_index("blk") * halos + lax.axis_index("head")) * tokens
    d_queries, d_keys, d_values, far_keys, far_values = attention(
        doc_lengths[0],
        base.astype(jnp.int32)[None],
        queries,
        grads,
        window[:, :width],
        window[:, width:],
        norms.reshape(groups, 1, -1),
        dots.T.reshape(groups, 1, -1),
        halos,
    )
    for back in range(1, halos + 1):
        rows = slice((halos - back) * tokens, (halos - back + 1) * tokens)
        far = shifted(jnp.concatenate([far_keys[rows], far_values[rows]], axis=1), -back)
        d_keys = d_keys + far[:, :width].astype(jnp.float32)
        d_values = d_values + far[:, width:].astype(jnp.float32)
    d_weight = jnp.concatenate([weight(index) for index in range(CHUNKS)], axis=0)
    return (
        d_queries[None],
        d_keys.astype(jnp.bfloat16)[None],
        d_values.astype(jnp.bfloat16)[None],
        d_weight,
    )


def solution(mesh):
    tokens = P("dp", ("blk", "head"), None)
    in_specs = (tokens, tokens, tokens, tokens, tokens, P("dp", "head", "blk"), tokens, P("dp", None))
    out_specs = (tokens, tokens, tokens, P("head", ("dp", "blk")))
    return jax.shard_map(shards, mesh=mesh, in_specs=in_specs, out_specs=out_specs, check_vma=False)
```

```python
import functools
import math

import jax
import jax.numpy as jnp
from jax import lax
from jax.experimental import pallas as pl
from jax.experimental.pallas import tpu as pltpu
from jax.sharding import PartitionSpec as P

HEAD_DIM = 128
CHUNKS = 4


def nt(left, right):
    return lax.dot_general(left, right, (((1,), (1,)), ((), ())), preferred_element_type=jnp.float32)


def tn(left, right):
    return lax.dot_general(left, right, (((0,), (0,)), ((), ())), preferred_element_type=jnp.float32)


def attention_kernel(
    halos, per_group, docs, lengths, base_ref, q_ref, g_ref, k_ref, v_ref, norm_ref, dots_ref,
    dq_ref, dk_ref, dv_ref, dk_far_ref, dv_far_ref, q_stack, g_stack, dq_acc
):
    tokens = q_ref.shape[0]
    base = base_ref[0]
    scale = 1.0 / math.sqrt(HEAD_DIM)
    for j in range(per_group):
        rows = slice(j * tokens, (j + 1) * tokens)
        cols = slice(j * HEAD_DIM, (j + 1) * HEAD_DIM)
        q_stack[rows, :] = q_ref[:, cols]
        g_stack[rows, :] = g_ref[:, cols]
    query_pos = base + lax.broadcasted_iota(jnp.int32, (tokens, tokens), 1)
    key_offset = lax.broadcasted_iota(jnp.int32, (tokens, tokens), 0)
    start = jnp.zeros((tokens, tokens), jnp.int32)
    first_start = jnp.int32(0)
    end = jnp.int32(0)
    for n in range(docs):
        end = end + lengths[n]
        start = jnp.where(query_pos >= end, end, start)
        first_start = jnp.where(base >= end, end, first_start)

    def block(back):
        rows = slice((halos - back) * tokens, (halos - back + 1) * tokens)
        key_pos = base - back * tokens + key_offset
        visible = (key_pos >= start) & (key_pos <= query_pos)
        visible = jnp.concatenate([visible.astype(jnp.float32)] * per_group, axis=1)
        keys = k_ref[rows, :]
        queries = q_stack[...]
        grads = g_stack[...]
        scores = nt(keys, queries) * scale
        probs = jnp.where(visible > 0.0, jnp.exp(scores - norm_ref[0]), 0.0)
        prob_grad = nt(v_ref[rows, :], grads)
        score_grad = (probs * (prob_grad - dots_ref[0]) * scale).astype(jnp.bfloat16)
        value_part = jnp.dot(probs.astype(jnp.bfloat16), grads, preferred_element_type=jnp.float32)
        key_part = jnp.dot(score_grad, queries, preferred_element_type=jnp.float32)
        return tn(score_grad, keys), key_part, value_part

    query_part, key_part, value_part = block(0)
    dq_acc[...] = query_part
    dk_ref[...] = key_part
    dv_ref[...] = value_part
    for back in range(1, halos + 1):
        rows = slice((halos - back) * tokens, (halos - back + 1) * tokens)
        near = base - back * tokens + tokens - 1 >= first_start

        @pl.when(near)
        def _(back=back, rows=rows):
            query_part, key_part, value_part = block(back)
            dq_acc[...] += query_part
            dk_far_ref[rows, :] = key_part.astype(dk_far_ref.dtype)
            dv_far_ref[rows, :] = value_part.astype(dv_far_ref.dtype)

        @pl.when(jnp.logical_not(near))
        def _(rows=rows):
            dk_far_ref[rows, :] = jnp.zeros((tokens, HEAD_DIM), dk_far_ref.dtype)
            dv_far_ref[rows, :] = jnp.zeros((tokens, HEAD_DIM), dv_far_ref.dtype)

    for j in range(per_group):
        rows = slice(j * tokens, (j + 1) * tokens)
        dq_ref[:, j * HEAD_DIM : (j + 1) * HEAD_DIM] = dq_acc[rows, :].astype(dq_ref.dtype)


def attention(lengths, base, queries, grads, keys, values, norms, dots, halos):
    tokens = queries.shape[0]
    groups = keys.shape[1] // HEAD_DIM
    per_group = queries.shape[1] // keys.shape[1]
    wide = per_group * HEAD_DIM
    body = functools.partial(attention_kernel, halos, per_group, lengths.shape[0])
    by_group = lambda g, *_: (0, g)
    stat = pl.BlockSpec((1, 1, per_group * tokens), lambda g, *_: (g, 0, 0))
    one = jax.ShapeDtypeStruct((tokens, groups * HEAD_DIM), jnp.float32)
    far = jax.ShapeDtypeStruct((halos * tokens, groups * HEAD_DIM), jnp.bfloat16)
    return pl.pallas_call(
        body,
        grid_spec=pltpu.PrefetchScalarGridSpec(
            num_scalar_prefetch=2,
            grid=(groups,),
            in_specs=[
                pl.BlockSpec((tokens, wide), by_group),
                pl.BlockSpec((tokens, wide), by_group),
                pl.BlockSpec((keys.shape[0], HEAD_DIM), by_group),
                pl.BlockSpec((keys.shape[0], HEAD_DIM), by_group),
                stat,
                stat,
            ],
            out_specs=[
                pl.BlockSpec((tokens, wide), by_group),
                pl.BlockSpec((tokens, HEAD_DIM), by_group),
                pl.BlockSpec((tokens, HEAD_DIM), by_group),
                pl.BlockSpec((halos * tokens, HEAD_DIM), by_group),
                pl.BlockSpec((halos * tokens, HEAD_DIM), by_group),
            ],
            scratch_shapes=[
                pltpu.VMEM((per_group * tokens, HEAD_DIM), jnp.bfloat16),
                pltpu.VMEM((per_group * tokens, HEAD_DIM), jnp.bfloat16),
                pltpu.VMEM((per_group * tokens, HEAD_DIM), jnp.float32),
            ],
        ),
        out_shape=[jax.ShapeDtypeStruct(queries.shape, jnp.bfloat16), one, one, far, far],
        compiler_params=pltpu.CompilerParams(vmem_limit_bytes=40 * 1024 * 1024),
        cost_estimate=pl.CostEstimate(
            flops=30_000_000_000, bytes_accessed=10_000_000, transcendentals=3_000_000
        ),
    )(lengths, base, queries, grads, keys, values, norms, dots)


def shifted(x, by):
    blocks, halves = lax.axis_size("blk"), lax.axis_size("head")
    place = lambda i: i % halves * blocks + i // halves
    count = blocks * halves
    pairs = [(place(i), place(i + by)) for i in range(count) if 0 <= i + by < count]
    return lax.ppermute(x, ("head", "blk"), pairs)


def shards(
    queries, keys, values, attention_output, output_gradient, saved_log_normaliser, proj_grad, doc_lengths
):
    halos = lax.axis_size("head")
    queries, keys, values = queries[0], keys[0], values[0]
    outputs, grads, cols_own = attention_output[0], output_gradient[0], proj_grad[0]
    tokens = queries.shape[0]
    groups = keys.shape[1] // HEAD_DIM
    heads = queries.shape[1] // HEAD_DIM

    rows_dp = lax.axis_size("dp")
    dp_order = [0]
    bits = [rows_dp >> n for n in range(1, rows_dp.bit_length())]
    for bit in bits:
        dp_order = dp_order + [other ^ bit for other in dp_order]
    dp_index, head_index = lax.axis_index("dp"), lax.axis_index("head")
    quarter = cols_own.shape[1] // rows_dp
    features = outputs.shape[1] // halos
    piece = features // CHUNKS

    def from_head(pick, head_index):
        return jnp.concatenate(
            [pick(head_index)]
            + [
                lax.ppermute(
                    pick((head_index + k) % halos), "head", [(i, (i + k) % halos) for i in range(halos)]
                )
                for k in range(1, halos)
            ],
            axis=0,
        )

    def flipped(x, bit):
        return lax.ppermute(x, "dp", [(i, i ^ bit) for i in range(rows_dp)])

    cols = from_head(lambda h: cols_own, head_index)
    cols = jnp.concatenate(
        [
            lax.dynamic_slice_in_dim(cols, (dp_index ^ other) * quarter, quarter, 1)
            if other == 0
            else flipped(lax.dynamic_slice_in_dim(cols, (dp_index ^ other) * quarter, quarter, 1), other)
            for other in dp_order
        ],
        axis=0,
    )

    def weight(index, head_index):
        part = from_head(
            lambda h: lax.dynamic_slice_in_dim(outputs, h * features + index * piece, piece, 1),
            head_index,
        )
        for bit in bits:
            part = jnp.concatenate([part, flipped(part, bit)], axis=0)
        part = tn(part, cols).astype(jnp.bfloat16)
        return lax.psum_scatter(part, "blk", scatter_dimension=1, tiled=True)

    both = jnp.concatenate([keys, values], axis=1)
    window = [shifted(both, back) for back in range(halos, 0, -1)] + [both]
    window = jnp.concatenate(window, axis=0)
    width = keys.shape[1]
    norms = lax.all_to_all(saved_log_normaliser[0], "head", split_axis=1, concat_axis=0, tiled=True)
    dots = jnp.sum(
        (grads.astype(jnp.float32) * outputs.astype(jnp.float32)).reshape(tokens, heads, HEAD_DIM), axis=2
    )
    base = (lax.axis_index("blk") * halos + lax.axis_index("head")) * tokens
    d_queries, d_keys, d_values, far_keys, far_values = attention(
        doc_lengths[0],
        base.astype(jnp.int32)[None],
        queries,
        grads,
        window[:, :width],
        window[:, width:],
        norms.reshape(groups, 1, -1),
        dots.T.reshape(groups, 1, -1),
        halos,
    )
    second_index, far_keys, far_values = lax.optimization_barrier((head_index, far_keys, far_values))
    for back in range(1, halos + 1):
        rows = slice((halos - back) * tokens, (halos - back + 1) * tokens)
        far = shifted(jnp.concatenate([far_keys[rows], far_values[rows]], axis=1), -back)
        d_keys = d_keys + far[:, :width].astype(jnp.float32)
        d_values = d_values + far[:, width:].astype(jnp.float32)
    later_index, d_keys, d_values = lax.optimization_barrier((second_index, d_keys, d_values))
    chosen = [head_index, second_index] + [later_index] * (CHUNKS - 2)
    d_weight = jnp.concatenate([weight(index, chosen[index]) for index in range(CHUNKS)], axis=0)
    return (
        d_queries[None],
        d_keys.astype(jnp.bfloat16)[None],
        d_values.astype(jnp.bfloat16)[None],
        d_weight,
    )


def solution(mesh):
    tokens = P("dp", ("blk", "head"), None)
    in_specs = (tokens, tokens, tokens, tokens, tokens, P("dp", "head", "blk"), tokens, P("dp", None))
    out_specs = (tokens, tokens, tokens, P("head", ("dp", "blk")))
    return jax.shard_map(shards, mesh=mesh, in_specs=in_specs, out_specs=out_specs, check_vma=False)
```
